512 devices in a mesh: ctx: 64 (over x, z, core), kvh: 8 (over y).
Axes of the slice: x: 4, y: 8, z: 8, core: 2. Of those that a mesh axis runs over, the one named last changes fastest.
Arguments:
- queries: bfloat16 [32768, 64, 128], P('ctx', 'kvh'), may hold values from -5 to 5
- keys: bfloat16 [32768, 8, 128], P('ctx', 'kvh'), may hold values from -5 to 5
- values: bfloat16 [32768, 8, 128], P('ctx', 'kvh'), may hold values from -6 to 6
- doc_ids: int32 [32768], replicated, may hold values from 0 to 31, never falling along the last dimension, each value on 1 to 2560 neighbouring positions
Outputs:
- attended: bfloat16 [32768, 8192], P(('ctx', 'kvh'))
The draws below stay inside these ranges and needn't reach their ends.
Inputs may be any that keep to these rules, and one draw needn't show every extreme that they name: `doc_ids`: document numbers never fall along the tokens; every document has 1 to 2560 tokens, and one has exactly that many.
All inputs are finite; a program needn't handle non-finite values.
Results may differ from the reference program's by a relative error of at most 0.0037.
Values may be sent and summed in bfloat16 or wider, within the bound.
No kernel may reach another device: no remote copies, remote signals or barrier semaphores. Data moves between devices by JAX's collectives and lax.ppermute only.
A program may use at most 64 MiB of HBM per device.

```python
import math
import jax
import jax.numpy as jnp
import numpy as np
from jax import lax

HD = 128
GROUP = 8
TOK_DEV = 512
SPAN = 5
KVH = 8
HEADS = 64
TOKENS = 32768


def draw_keys(key, part):
    key = jax.random.fold_in(key, 3)
    result = jnp.clip(jax.random.normal(key, (TOKENS, KVH, HD), jnp.float32), -5.0, 5.0)
    return result.astype(jnp.bfloat16)


def draw_queries(key, part):
    key = jax.random.fold_in(key, 7)
    result = jnp.clip(jax.random.normal(key, (TOKENS, HEADS, HD), jnp.float32), -5.0, 5.0)
    return result.astype(jnp.bfloat16)


def level_of(rng, dims, shards, low, top_value):
    factor_of = 1.0
    for axis_at, parts in shards:
        steps = jax.random.uniform(jax.random.fold_in(jax.random.fold_in(rng, 6), axis_at), (parts,), jnp.float32, low / len(shards), top_value / len(shards))
        factor_of = factor_of * jnp.repeat(jnp.exp(steps), dims[axis_at] // parts).reshape((-1,) + (1,) * (len(dims) - 1 - axis_at))
    return factor_of


def profile(amount, total, limit, lean):
    weights = [(1 << 20) // math.isqrt(standing ** lean) + 1 for standing in range(2, amount + 1)]
    spare, counts = total - limit - (amount - 1), [1] * (amount - 1)
    while spare > 0:
        movable = [i for i in range(amount - 1) if counts[i] < limit]
        mass, remaining = sum([weights[i] for i in movable]), spare
        for i in movable:
            addition = min(limit - counts[i], max(1, remaining * weights[i] // mass), spare)
            counts[i] = counts[i] + addition
            spare = spare - addition
    return np.array([limit] + counts)


def uneven(key, number_of, total, bound, slope):
    if number_of == 2:
        one = jax.random.randint(key, (), max(1, total - bound), min(bound, total - 1) + 1)
        return jnp.stack([one, total - one])
    sizes = jnp.asarray(profile(number_of, total, bound, slope), jnp.int32)
    pairs = (number_of - 1) // 2
    giver, sink = sizes[1:1 + 2 * pairs:2], sizes[2:2 + 2 * pairs:2]
    room = jnp.minimum(giver - 1, bound - sink)
    passed = jax.random.randint(jax.random.fold_in(key, 1), (pairs,), 0, 1 << 20) % (room + 1)
    sizes = sizes.at[1:1 + 2 * pairs:2].set(giver - passed).at[2:2 + 2 * pairs:2].set(sink + passed)
    return sizes[jax.random.permutation(jax.random.fold_in(key, 2), number_of)]


def bell_draw(own_key, dims, spread, bound, pieces=(), kind=jnp.bfloat16):
    loudness = level_of(own_key, dims, pieces, -0.22, 0.18) if pieces else 1.0
    values = jax.random.normal(own_key, dims, jnp.float32) * spread * loudness
    return jnp.minimum(jnp.maximum(values, -bound), bound).astype(kind)


def setup_inputs(seed: int = 0) -> dict:
    seeds = jax.random.split(jax.random.key(seed), 5)
    return {
        "queries": draw_queries(jax.random.fold_in(seeds[4], 71), 0),
        "keys": draw_keys(jax.random.fold_in(seeds[4], 71), 0),
        "values": bell_draw(seeds[2], (TOKENS, KVH, HD), 1.0, 6.0, ((0, 64), (1, 8))),
        "doc_ids": jnp.searchsorted(jnp.cumsum(uneven(seeds[3], TOKENS // (2 * TOK_DEV), TOKENS, SPAN * TOK_DEV, 1)), jnp.arange(TOKENS), side="right").astype(jnp.int32),
    }


def reference(queries, keys, values, doc_ids):
    lead = SPAN * TOK_DEV
    key_width = (SPAN + 1) * TOK_DEV
    keys_pad = jnp.concatenate([jnp.zeros((lead, KVH, HD), keys.dtype), keys], 0)
    values_pad = jnp.concatenate([jnp.zeros((lead, KVH, HD), values.dtype), values], 0)
    docs_pad = jnp.concatenate([jnp.full((lead,), -1, jnp.int32), doc_ids.astype(jnp.int32)])
    score_scale = 1.0 / math.sqrt(HD)

    def one_block(block_index):
        start = (block_index * TOK_DEV).astype(jnp.int32)
        query_rows = lax.dynamic_slice_in_dim(queries, start, TOK_DEV, 0).astype(jnp.float32)
        query_rows = query_rows.reshape(TOK_DEV, KVH, GROUP, HD)
        key_rows = lax.dynamic_slice_in_dim(keys_pad, start, key_width, 0).astype(jnp.float32)
        value_rows = lax.dynamic_slice_in_dim(values_pad, start, key_width, 0).astype(jnp.float32)
        key_docs = lax.dynamic_slice_in_dim(docs_pad, start, key_width, 0)
        query_docs = lax.dynamic_slice_in_dim(doc_ids.astype(jnp.int32), start, TOK_DEV, 0)
        key_pos = start - lead + jnp.arange(key_width, dtype=jnp.int32)
        query_pos = start + jnp.arange(TOK_DEV, dtype=jnp.int32)
        allowed = (query_docs[:, None] == key_docs[None, :]) & (key_pos[None, :] <= query_pos[:, None])

        def one_head(kv_head):
            query_head = query_rows[:, kv_head]
            key_head = key_rows[:, kv_head]
            value_head = value_rows[:, kv_head]
            scores = jnp.einsum('tgd,kd->gtk', query_head, key_head) * score_scale
            scores = jnp.where(allowed[None], scores, -1e+30)
            row_max = lax.optimization_barrier(jnp.max(scores, axis=2, keepdims=True))
            raised = jnp.exp(scores - row_max)
            row_total = lax.optimization_barrier(jnp.sum(raised, axis=2, keepdims=True))
            weights_bf = lax.optimization_barrier(raised.astype(jnp.bfloat16))
            weighted = jnp.einsum('gtk,kd->gtd', weights_bf.astype(jnp.float32), value_head) / row_total
            return weighted.astype(jnp.bfloat16)
        per_head = lax.map(one_head, jnp.arange(KVH, dtype=jnp.int32))
        return jnp.transpose(per_head, (2, 0, 1, 3)).reshape(TOK_DEV, KVH * GROUP * HD)
    blocks = lax.map(one_block, jnp.arange(TOKENS // TOK_DEV, dtype=jnp.int32))
    return blocks.reshape(TOKENS, KVH * GROUP * HD)
```

```python
import functools
import math

import jax
import jax.numpy as jnp
from jax import lax
from jax.experimental import pallas as pl
from jax.experimental.pallas import tpu as pltpu
from jax.sharding import PartitionSpec as P

SPAN = 5
ONES = 8
COST = 1000
LAG = 3
VMEM = pl.BlockSpec(memory_space=pltpu.VMEM)
SMEM = pl.BlockSpec(memory_space=pltpu.SMEM)
ANY = pl.BlockSpec(memory_space=pl.ANY)
PARAMS = pltpu.CompilerParams(vmem_limit_bytes=32 * 2**20)
bf16, f32, i32 = jnp.bfloat16, jnp.float32, jnp.int32


def hop(value, steps):
    count = lax.axis_size("ctx")
    return lax.ppermute(value, "ctx", [(i, i + steps) for i in range(count - steps)])


def swap_cores(value):
    count = lax.axis_size("ctx")
    return lax.ppermute(value, "ctx", [(i, i ^ 1) for i in range(count)])


def turn(value, steps):
    count = lax.axis_size("kvh")
    return lax.ppermute(value, "kvh", [(i, (i + steps) % count) for i in range(count)])


def values_kernel(kv_ref, out_ref):
    tok = kv_ref.shape[0] // 2
    dim = kv_ref.shape[1]
    out_ref[:dim, :] = kv_ref[tok:, :].T
    out_ref[dim:, :] = jnp.ones((ONES, tok), bf16)


def turned_values(kv):
    tok, dim = kv.shape[0] // 2, kv.shape[1]
    return pl.pallas_call(
        values_kernel,
        in_specs=[VMEM],
        out_specs=VMEM,
        out_shape=jax.ShapeDtypeStruct((dim + ONES, tok), bf16),
        compiler_params=PARAMS,
        cost_estimate=pl.CostEstimate(flops=0, bytes_accessed=4 * tok * dim, transcendentals=0),
        name="values_turned",
    )(kv)


def chunk_kernel(at_ref, qt_ref, first_ref, k_ref, vt_ref, after_ref, other_ref, out_ref, *, tok, heads, part, window):
    chunk = at_ref[0]
    rows = qt_ref.shape[2]
    dim = k_ref.shape[1]
    scale = math.log2(math.e) / math.sqrt(dim)
    base = pl.multiple_of(chunk * part // 128 * 128, 128)
    keys = k_ref[pl.ds(base, window), :]
    scores = jnp.dot(keys, qt_ref[chunk], preferred_element_type=f32) * scale
    first = first_ref[chunk] - base
    own = SPAN * tok + chunk * part - base
    own = own + (lax.broadcasted_iota(i32, (1, rows), 1) & (part - 1))
    key = lax.broadcasted_iota(i32, (window, rows), 0)
    allowed = (key - first).astype(jnp.uint32) <= (own - first).astype(jnp.uint32)
    scores = jnp.where(allowed, scores, -1e30)
    row_max = jnp.max(scores, axis=0, keepdims=True)
    raised = jnp.exp2(scores - row_max)
    total = jnp.dot(
        vt_ref[:, pl.ds(base, window)], raised.astype(bf16), preferred_element_type=f32
    )
    result = (total[:dim] / total[dim : dim + 1]).T.astype(bf16)
    for head in range(heads):
        out_ref[:, head * dim : (head + 1) * dim] = result[head * part : (head + 1) * part]


def attend_chunk(at, qt, first, keys, vt, after, other, tok, heads, part):
    dim = keys.shape[1]
    rows = qt.shape[2]
    window = (SPAN * tok + part + 127) // 128 * 128
    window = window + (128 if part % 128 == 0 else 0)
    window = min(window, keys.shape[0])
    return pl.pallas_call(
        functools.partial(
            chunk_kernel, tok=tok, heads=heads, part=part, window=window
        ),
        in_specs=[SMEM, VMEM, VMEM, VMEM, VMEM, ANY, ANY],
        out_specs=VMEM,
        out_shape=jax.ShapeDtypeStruct((part, heads * dim), bf16),
        compiler_params=PARAMS,
        cost_estimate=pl.CostEstimate(flops=COST, bytes_accessed=0, transcendentals=0),
        name="attend_chunk",
    )(at, qt, first, keys, vt, after, other)


def gather_kernel(source_ref, *refs):
    *pieces, out_ref, sems = refs
    width = pieces[0].shape[1]
    copies = []
    for i, piece in enumerate(pieces):
        place = pl.ds(pl.multiple_of(source_ref[i] * width, 128), width)
        copies.append(pltpu.make_async_copy(piece, out_ref.at[:, place], sems.at[i]))
    for copy in copies:
        copy.start()
    for copy in copies:
        copy.wait()


def gather_pieces(sources, pieces):
    part, width = pieces[0].shape
    count = len(pieces)
    return pl.pallas_call(
        gather_kernel,
        in_specs=[SMEM] + [VMEM] * count,
        out_specs=pl.BlockSpec(memory_space=pl.ANY),
        out_shape=jax.ShapeDtypeStruct((part, count * width), bf16),
        scratch_shapes=[pltpu.SemaphoreType.DMA((count,))],
        compiler_params=PARAMS,
        cost_estimate=pl.CostEstimate(flops=0, bytes_accessed=0, transcendentals=0),
        name="gather_pieces",
    )(sources, *pieces)


def on_device(queries, keys, values, doc_ids):
    tok, heads, dim = queries.shape
    ring = lax.axis_size("kvh")
    part = tok // ring
    me = lax.axis_index("kvh")
    own_index = lax.axis_index("ctx")
    first_core = own_index % 2 == 0

    kv0 = jnp.concatenate([keys[:, 0], values[:, 0]], 0)
    kv2 = hop(kv0, 2)
    kv1 = swap_cores(jnp.where(first_core, kv0, kv2))
    kv4 = hop(kv2, 2)
    kv3 = swap_cores(jnp.where(first_core, kv2, kv4))
    kv5 = hop(kv4, 1)
    blocks = [kv5, kv4, kv3, kv2, kv1, kv0]

    width = (SPAN + 1) * tok
    padded = jnp.concatenate([jnp.full((SPAN * tok,), -1, i32), doc_ids])
    near = lax.dynamic_slice_in_dim(padded, own_index * tok, width, 0)
    mine = near[SPAN * tok :]
    first = jnp.sum((near[None, :] < mine[:, None]).astype(i32), axis=1)
    first = jnp.tile(first.reshape(ring, 1, part), (1, 1, heads))

    qt = queries.reshape(ring, part, heads, dim).transpose(0, 3, 2, 1)
    qt = qt.reshape(ring, dim, heads * part)
    all_keys = jnp.concatenate([b[:tok] for b in blocks], 0)
    vt = jnp.concatenate([turned_values(b) for b in blocks], 1)

    order = (4, 3, 5, 2, 6, 1, 7, 0)
    pieces, piece = [], vt
    for i, steps in enumerate(order):
        at = ((me + steps) % ring).astype(i32).reshape(1)
        other = pieces[i - LAG] if i >= LAG else vt
        piece = attend_chunk(at, qt, first, all_keys, vt, piece, other, tok, heads, part)
        pieces.append(turn(piece, steps) if steps else piece)
    sources = jnp.stack([(me - steps) % ring for steps in order]).astype(i32)
    return gather_pieces(sources, pieces)


def solution(mesh):
    in_specs = (P("ctx", "kvh", None), P("ctx", "kvh", None), P("ctx", "kvh", None), P())
    out_specs = P(("ctx", "kvh"), None)
    return jax.shard_map(
        on_device, mesh=mesh, in_specs=in_specs, out_specs=out_specs, check_vma=False
    )
```

```python
import functools
import math

import jax
import jax.numpy as jnp
from jax import lax
from jax.experimental import pallas as pl
from jax.experimental.pallas import tpu as pltpu
from jax.sharding import PartitionSpec as P

SPAN = 5
ONES = 8
COST = 1000
VMEM = pl.BlockSpec(memory_space=pltpu.VMEM)
SMEM = pl.BlockSpec(memory_space=pltpu.SMEM)
ANY = pl.BlockSpec(memory_space=pl.ANY)
PARAMS = pltpu.CompilerParams(vmem_limit_bytes=32 * 2**20)
bf16, f32, i32 = jnp.bfloat16, jnp.float32, jnp.int32


def hop(value, steps):
    count = lax.axis_size("ctx")
    return lax.ppermute(value, "ctx", [(i, i + steps) for i in range(count - steps)])


def swap_cores(value):
    count = lax.axis_size("ctx")
    return lax.ppermute(value, "ctx", [(i, i ^ 1) for i in range(count)])


def scores_of(keys, qt):
    scale = math.log2(math.e) / math.sqrt(keys.shape[1])
    return jnp.dot(keys, qt, preferred_element_type=f32) * scale


def own_kernel(qt_ref, first_ref, kv_ref, acc_ref, max_ref, vt_ref, *, part):
    chunks, dim, rows = qt_ref.shape
    tok = kv_ref.shape[0] // 2
    vt_ref[:dim, :] = kv_ref[tok:, :].T
    vt_ref[dim:, :] = jnp.ones((ONES, tok), bf16)
    place = lax.broadcasted_iota(i32, (1, rows), 1) & (part - 1)
    for chunk in range(chunks):
        width = min(tok, (chunk * part + part + 127) // 128 * 128)
        scores = scores_of(kv_ref[:width, :], qt_ref[chunk])
        first = first_ref[chunk] - SPAN * tok
        own = chunk * part + place
        key = lax.broadcasted_iota(i32, (width, rows), 0)
        scores = jnp.where((key >= first) & (key <= own), scores, -1e30)
        row_max = jnp.max(scores, axis=0, keepdims=True)
        raised = jnp.exp2(scores - row_max).astype(bf16)
        acc_ref[chunk] = jnp.dot(vt_ref[:, :width], raised, preferred_element_type=f32)
        max_ref[chunk] = row_max


def earlier_kernel(ends_ref, qt_ref, first_ref, *refs, base, part, last):
    count = len(refs) - (5 if last else 6)
    blocks, rest = refs[:count], refs[count:]
    if last:
        acc_in, max_in, out_ref, keys_ref, vt_ref = rest
    else:
        acc_in, max_in, acc_out, max_out, keys_ref, vt_ref = rest
    chunks, dim, rows = qt_ref.shape
    tok = blocks[0].shape[0] // 2
    width = count * tok
    for i, block in enumerate(blocks):
        keys_ref[i * tok : (i + 1) * tok, :] = block[:tok, :]
        vt_ref[:dim, i * tok : (i + 1) * tok] = block[tok:, :].T
    vt_ref[dim:, :] = jnp.ones((ONES, width), bf16)

    def step(chunk, masked):
        scores = scores_of(keys_ref[...], qt_ref[chunk])
        if masked:
            key = base + lax.broadcasted_iota(i32, (width, rows), 0)
            scores = jnp.where(key >= first_ref[chunk], scores, -1e30)
        old = max_in[chunk]
        new = jnp.maximum(old, jnp.max(scores, axis=0, keepdims=True))
        raised = jnp.exp2(scores - new).astype(bf16)
        part_sum = jnp.dot(vt_ref[...], raised, preferred_element_type=f32)
        total = acc_in[chunk] * jnp.exp2(old - new) + part_sum
        if last:
            finish(chunk, total)
        else:
            acc_out[chunk] = total
            max_out[chunk] = new

    def finish(chunk, total):
        result = (total[:dim] / total[dim : dim + 1]).T.astype(bf16)
        for head in range(rows // part):
            out_ref[chunk, :, head * dim : (head + 1) * dim] = result[
                head * part : (head + 1) * part
            ]

    def body(chunk, carry):
        whole = base >= ends_ref[1, chunk]
        none = base + width <= ends_ref[0, chunk]

        @pl.when(whole)
        def _():
            step(chunk, False)

        @pl.when(jnp.logical_not(whole | none))
        def _():
            step(chunk, True)

        @pl.when(none)
        def _():
            if last:
                finish(chunk, acc_in[chunk])
            else:
                acc_out[chunk] = acc_in[chunk]
                max_out[chunk] = max_in[chunk]

        return carry

    lax.fori_loop(0, chunks, body, 0)


def attend_own(qt, first, kv, part):
    chunks, dim, rows = qt.shape
    tok = kv.shape[0] // 2
    return pl.pallas_call(
        functools.partial(own_kernel, part=part),
        in_specs=[VMEM] * 3,
        out_specs=[VMEM] * 2,
        out_shape=[
            jax.ShapeDtypeStruct((chunks, dim + ONES, rows), f32),
            jax.ShapeDtypeStruct((chunks, 1, rows), f32),
        ],
        scratch_shapes=[pltpu.VMEM((dim + ONES, tok), bf16)],
        compiler_params=PARAMS,
        cost_estimate=pl.CostEstimate(flops=COST, bytes_accessed=0, transcendentals=0),
        name="attend_own",
    )(qt, first, kv)


def attend_earlier(ends, qt, first, blocks, base, state, part, last=False):
    chunks, dim, rows = qt.shape
    tok = blocks[0].shape[0] // 2
    width = len(blocks) * tok
    acc, row_max = state
    if last:
        out_shape = jax.ShapeDtypeStruct((chunks, part, rows // part * dim), bf16)
        out_specs, alias = VMEM, {}
    else:
        out_shape = [jax.ShapeDtypeStruct(a.shape, f32) for a in state]
        out_specs = [VMEM] * 2
        alias = {3 + len(blocks): 0, 4 + len(blocks): 1}
    return pl.pallas_call(
        functools.partial(earlier_kernel, base=base, part=part, last=last),
        in_specs=[SMEM] + [VMEM] * (4 + len(blocks)),
        out_specs=out_specs,
        out_shape=out_shape,
        input_output_aliases=alias,
        scratch_shapes=[
            pltpu.VMEM((width, dim), bf16),
            pltpu.VMEM((dim + ONES, width), bf16),
        ],
        compiler_params=PARAMS,
        cost_estimate=pl.CostEstimate(flops=COST, bytes_accessed=0, transcendentals=0),
        name="attend_earlier",
    )(ends, qt, first, *blocks, acc, row_max)


def gate(value, after):
    return pl.pallas_call(
        lambda value_ref, after_ref, out_ref: None,
        in_specs=[ANY] * 2,
        out_specs=ANY,
        out_shape=jax.ShapeDtypeStruct(value.shape, value.dtype),
        input_output_aliases={0: 0},
        cost_estimate=pl.CostEstimate(flops=0, bytes_accessed=0, transcendentals=0),
        name="gate",
    )(value, after)


def on_device(queries, keys, values, doc_ids):
    tok, heads, dim = queries.shape
    ring = lax.axis_size("kvh")
    part = tok // ring
    own_index = lax.axis_index("ctx")
    first_core = own_index % 2 == 0

    width = (SPAN + 1) * tok
    padded = jnp.concatenate([jnp.full((SPAN * tok,), -1, i32), doc_ids])
    near = lax.dynamic_slice_in_dim(padded, own_index * tok, width, 0)
    mine = near[SPAN * tok :]
    begins = jnp.sum((near[None, :] < mine[:, None]).astype(i32), axis=1)
    ends = jnp.stack([begins[::part], begins[part - 1 :: part]])
    first = jnp.tile(begins.reshape(ring, 1, part), (1, 1, heads))

    qt = queries.reshape(ring, part, heads, dim).transpose(0, 3, 2, 1)
    qt = qt.reshape(ring, dim, heads * part)

    kv0 = jnp.concatenate([keys[:, 0], values[:, 0]], 0)
    kv2 = hop(kv0, 2)
    state = attend_own(qt, first, kv0, part)
    kv2 = gate(kv2, state[1])
    kv4 = hop(kv2, 2)
    kv1 = swap_cores(jnp.where(first_core, kv0, kv2))
    state = attend_earlier(ends, qt, first, [kv2, kv1], 3 * tok, state, part)
    kv4 = gate(kv4, state[1])
    kv5 = hop(kv4, 1)
    kv3 = swap_cores(jnp.where(first_core, kv2, kv4))
    state = attend_earlier(ends, qt, first, [kv4, kv3], tok, state, part)
    pieces = attend_earlier(ends, qt, first, [kv5], 0, state, part, last=True)
    pieces = lax.all_to_all(pieces, "kvh", split_axis=0, concat_axis=0, tiled=True)
    return pieces.transpose(1, 0, 2).reshape(part, ring * heads * dim)


def solution(mesh):
    in_specs = (P("ctx", "kvh", None), P("ctx", "kvh", None), P("ctx", "kvh", None), P())
    out_specs = P(("ctx", "kvh"), None)
    return jax.shard_map(
        on_device, mesh=mesh, in_specs=in_specs, out_specs=out_specs, check_vma=False
    )
```

```python
import functools
import math

import jax
import jax.numpy as jnp
from jax import lax
from jax.experimental import pallas as pl
from jax.experimental.pallas import tpu as pltpu
from jax.sharding import PartitionSpec as P

SPAN = 5
ONES = 8
ROOM = 100.0
VMEM = pl.BlockSpec(memory_space=pltpu.VMEM)
SMEM = pl.BlockSpec(memory_space=pltpu.SMEM)
ANY = pl.BlockSpec(memory_space=pl.ANY)
PARAMS = pltpu.CompilerParams(vmem_limit_bytes=16 * 2**20)
COST = pl.CostEstimate(flops=1000, bytes_accessed=0, transcendentals=0)
bf16, f32, i32 = jnp.bfloat16, jnp.float32, jnp.int32


def hop(value, steps):
    count = lax.axis_size("ctx")
    return lax.ppermute(value, "ctx", [(i, i + steps) for i in range(count - steps)])


def swap_cores(value):
    count = lax.axis_size("ctx")
    return lax.ppermute(value, "ctx", [(i, i ^ 1) for i in range(count)])


def scores_of(keys, qt):
    scale = math.log2(math.e) / math.sqrt(keys.shape[1])
    return jnp.dot(keys, qt, preferred_element_type=f32) * scale


def own_kernel(qt_ref, first_ref, kv_ref, acc_ref, max_ref, bound_ref, vt_ref, *, part):
    chunks, dim, rows = qt_ref.shape
    tok = kv_ref.shape[0] // 2
    vt_ref[:dim, :] = kv_ref[tok:, :].T
    vt_ref[dim:, :] = jnp.ones((ONES, tok), bf16)
    place = lax.broadcasted_iota(i32, (1, rows), 1) & (part - 1)
    largest = jnp.zeros((1, rows), f32)
    lowest = jnp.full((1, rows), jnp.inf, f32)
    for chunk in range(chunks):
        width = min(tok, (chunk * part + part + 127) // 128 * 128)
        scores = scores_of(kv_ref[:width, :], qt_ref[chunk])
        first = first_ref[chunk] - SPAN * tok
        own = chunk * part + place
        key = lax.broadcasted_iota(i32, (width, rows), 0)
        scores = jnp.where((key >= first) & (key <= own), scores, -1e30)
        row_max = jnp.max(scores, axis=0, keepdims=True)
        raised = jnp.exp2(scores - row_max).astype(bf16)
        acc_ref[chunk] = jnp.dot(vt_ref[:, :width], raised, preferred_element_type=f32)
        max_ref[chunk] = row_max
        squares = jnp.square(qt_ref[chunk].astype(f32))
        largest = jnp.maximum(largest, jnp.sum(squares, axis=0, keepdims=True))
        lowest = jnp.minimum(lowest, row_max)
    bound_ref[0:1] = largest
    bound_ref[1:2] = lowest


def earlier_kernel(qt_ref, first_ref, bound_ref, *refs, base, part, last):
    count = len(refs) - (5 if last else 6)
    blocks, rest = refs[:count], refs[count:]
    if last:
        acc_in, max_in, out_ref, keys_ref, vt_ref = rest
    else:
        acc_in, max_in, acc_out, max_out, keys_ref, vt_ref = rest
    chunks, dim, rows = qt_ref.shape
    tok = blocks[0].shape[0] // 2
    width = count * tok
    end = base + width

    def leave(chunk, total, row_max):
        if last:
            result = (total[:dim] / total[dim : dim + 1]).T.astype(bf16)
            for head in range(rows // part):
                out_ref[chunk, :, head * dim : (head + 1) * dim] = result[
                    head * part : (head + 1) * part
                ]
        else:
            acc_out[chunk] = total
            max_out[chunk] = row_max

    def step(chunk, masked, raising):
        scores = scores_of(keys_ref[...], qt_ref[chunk])
        if masked:
            key = base + lax.broadcasted_iota(i32, (width, rows), 0)
            scores = jnp.where(key >= first_ref[chunk], scores, -1e30)
        old = new = max_in[chunk]
        total = acc_in[chunk]
        if raising:
            new = jnp.maximum(old, jnp.max(scores, axis=0, keepdims=True))
            total = total * jnp.exp2(old - new)
        raised = jnp.exp2(scores - new).astype(bf16)
        total = total + jnp.dot(vt_ref[...], raised, preferred_element_type=f32)
        leave(chunk, total, new)

    lowest_first, highest_first = jnp.min(first_ref[...]), jnp.max(first_ref[...])
    needed = lowest_first < end

    @pl.when(jnp.logical_not(needed))
    def _():
        for chunk in range(chunks):
            leave(chunk, acc_in[chunk], max_in[chunk])

    @pl.when(needed)
    def _():
        for i, block in enumerate(blocks):
            keys_ref[i * tok : (i + 1) * tok, :] = block[:tok, :]
            vt_ref[:dim, i * tok : (i + 1) * tok] = block[tok:, :].T
        vt_ref[dim:, :] = jnp.ones((ONES, width), bf16)
        squares = jnp.square(keys_ref[...].astype(f32))
        key_bound = jnp.max(jnp.sum(squares, axis=1, keepdims=True))
        query_bound = jnp.max(bound_ref[0:1])
        slack = jnp.min(bound_ref[1:2]) + ROOM
        scale = math.log2(math.e) ** 2 / dim * 1.01
        small = (slack > 0) & (query_bound * key_bound * scale <= slack * slack)
        plain = small & (highest_first <= base)

        @pl.when(plain)
        def _():
            for chunk in range(chunks):
                step(chunk, False, False)

        @pl.when(jnp.logical_not(plain))
        def _():
            def body(chunk, carry):
                low, high = jnp.min(first_ref[chunk]), jnp.max(first_ref[chunk])
                some = low < end
                part_of = high > base

                @pl.when(jnp.logical_not(some))
                def _():
                    leave(chunk, acc_in[chunk], max_in[chunk])

                @pl.when(some & small & part_of)
                def _():
                    step(chunk, True, False)

                @pl.when(some & small & jnp.logical_not(part_of))
                def _():
                    step(chunk, False, False)

                @pl.when(some & jnp.logical_not(small))
                def _():
                    step(chunk, True, True)

                return carry

            lax.fori_loop(0, chunks, body, 0)


def attend_own(qt, first, kv, part):
    chunks, dim, rows = qt.shape
    tok = kv.shape[0] // 2
    return pl.pallas_call(
        functools.partial(own_kernel, part=part),
        in_specs=[VMEM] * 3,
        out_specs=[VMEM] * 3,
        out_shape=[
            jax.ShapeDtypeStruct((chunks, dim + ONES, rows), f32),
            jax.ShapeDtypeStruct((chunks, 1, rows), f32),
            jax.ShapeDtypeStruct((2, rows), f32),
        ],
        scratch_shapes=[pltpu.VMEM((dim + ONES, tok), bf16)],
        compiler_params=PARAMS,
        cost_estimate=COST,
        name="attend_own",
    )(qt, first, kv)


def attend_earlier(qt, first, bound, blocks, base, state, part, last=False):
    chunks, dim, rows = qt.shape
    tok = blocks[0].shape[0] // 2
    width = len(blocks) * tok
    acc, row_max = state
    if last:
        out_shape = jax.ShapeDtypeStruct((chunks, part, rows // part * dim), bf16)
        out_specs, alias = VMEM, {}
    else:
        out_shape = [jax.ShapeDtypeStruct(a.shape, f32) for a in state]
        out_specs = [VMEM] * 2
        alias = {3 + len(blocks): 0, 4 + len(blocks): 1}
    return pl.pallas_call(
        functools.partial(earlier_kernel, base=base, part=part, last=last),
        in_specs=[VMEM] * (5 + len(blocks)),
        out_specs=out_specs,
        out_shape=out_shape,
        input_output_aliases=alias,
        scratch_shapes=[
            pltpu.VMEM((width, dim), bf16),
            pltpu.VMEM((dim + ONES, width), bf16),
        ],
        compiler_params=PARAMS,
        cost_estimate=COST,
        name="attend_earlier",
    )(qt, first, bound, *blocks, acc, row_max)


def pass_kernel(second_ref, near_ref, far_ref, after_ref, on_ref, other_ref):
    on_ref[...] = far_ref[...]

    @pl.when(second_ref[0] == 0)
    def _():
        other_ref[...] = near_ref[...]

    @pl.when(second_ref[0] != 0)
    def _():
        other_ref[...] = far_ref[...]


def pass_on(second, near, far, after):
    return pl.pallas_call(
        pass_kernel,
        in_specs=[SMEM, VMEM, VMEM, ANY],
        out_specs=[VMEM] * 2,
        out_shape=[jax.ShapeDtypeStruct(far.shape, far.dtype)] * 2,
        input_output_aliases={2: 0},
        compiler_params=PARAMS,
        cost_estimate=COST,
        name="pass_on",
    )(second, near, far, after)


def on_device(queries, keys, values, doc_ids):
    tok, heads, dim = queries.shape
    ring = lax.axis_size("kvh")
    part = tok // ring
    own_index = lax.axis_index("ctx")
    second = (own_index % 2).astype(i32).reshape(1)

    width = (SPAN + 1) * tok
    padded = jnp.concatenate([jnp.full((SPAN * tok,), -1, i32), doc_ids])
    near = lax.dynamic_slice_in_dim(padded, own_index * tok, width, 0)
    mine = near[SPAN * tok :]
    begins = jnp.sum((near[None, :] < mine[:, None]).astype(i32), axis=1)
    first = jnp.tile(begins.reshape(ring, 1, part), (1, 1, heads))

    qt = queries.reshape(ring, part, heads, dim).transpose(0, 3, 2, 1)
    qt = qt.reshape(ring, dim, heads * part)

    kv0 = jnp.concatenate([keys[:, 0], values[:, 0]], 0)
    kv2 = hop(kv0, 2)
    acc, row_max, bound = attend_own(qt, first, kv0, part)
    kv2, other = pass_on(second, kv0, kv2, row_max)
    kv4 = hop(kv2, 2)
    kv1 = swap_cores(other)
    acc, row_max = attend_earlier(qt, first, bound, [kv2, kv1], 3 * tok, (acc, row_max), part)
    kv4, other = pass_on(second, kv2, kv4, row_max)
    kv5 = hop(kv4, 1)
    kv3 = swap_cores(other)
    acc, row_max = attend_earlier(qt, first, bound, [kv4, kv3], tok, (acc, row_max), part)
    pieces = attend_earlier(qt, first, bound, [kv5], 0, (acc, row_max), part, last=True)
    pieces = lax.all_to_all(pieces, "kvh", split_axis=0, concat_axis=0, tiled=True)
    return pieces.transpose(1, 0, 2).reshape(part, ring * heads * dim)


def solution(mesh):
    in_specs = (P("ctx", "kvh", None), P("ctx", "kvh", None), P("ctx", "kvh", None), P())
    out_specs = P(("ctx", "kvh"), None)
    return jax.shard_map(
        on_device, mesh=mesh, in_specs=in_specs, out_specs=out_specs, check_vma=False
    )
```

```python
import functools
import math

import jax
import jax.numpy as jnp
from jax import lax
from jax.experimental import pallas as pl
from jax.experimental.pallas import tpu as pltpu
from jax.sharding import PartitionSpec as P

SPAN = 5
DOCS = 32
EXTRA = 8
ROOM = 100.0
VMEM = pl.BlockSpec(memory_space=pltpu.VMEM)
ANY = pl.BlockSpec(memory_space=pl.ANY)
PARAMS = pltpu.CompilerParams(vmem_limit_bytes=16 * 2**20)
COST = pl.CostEstimate(flops=1000, bytes_accessed=0, transcendentals=0)
bf16, f32, i32 = jnp.bfloat16, jnp.float32, jnp.int32


def hop(value, steps):
    count = lax.axis_size("ctx")
    return lax.ppermute(value, "ctx", [(i, i + steps) for i in range(count - steps)])


def scores_of(keys, qt):
    scale = math.log2(math.e) / math.sqrt(keys.shape[1])
    return jnp.dot(keys, qt, preferred_element_type=f32) * scale


def one_row(width):
    return (lax.broadcasted_iota(i32, (EXTRA, width), 0) == 0).astype(bf16)


def own_kernel(qt_ref, near_ref, kv_ref, state_ref, done_ref, vt_ref, *, part):
    chunks, dim, rows = qt_ref.shape
    tok = kv_ref.shape[0] // 2
    lanes = near_ref.shape[1]
    vt_ref[:dim, :] = kv_ref[tok:, :].T
    vt_ref[dim:, :] = one_row(tok)

    near = near_ref[...]
    mine = near[SPAN * tok // lanes :]
    begins = jnp.zeros(mine.shape, i32)
    for doc in range(DOCS):
        before = jnp.sum((near < doc).astype(f32), axis=(0, 1), keepdims=True)
        begins = jnp.where(mine == doc, before.astype(i32), begins)

    place = lax.broadcasted_iota(i32, (1, rows), 1) & (part - 1)
    for chunk in range(chunks):
        at, lane = divmod(chunk * part, lanes)
        first = jnp.concatenate([begins[at : at + 1, lane : lane + part]] * (rows // part), 1)
        width = min(tok, (chunk * part + part + 127) // 128 * 128)
        scores = scores_of(kv_ref[:width, :], qt_ref[chunk])
        own = chunk * part + place
        key = lax.broadcasted_iota(i32, (width, rows), 0)
        scores = jnp.where((key >= first - SPAN * tok) & (key <= own), scores, -1e30)
        row_max = jnp.max(scores, axis=0, keepdims=True)
        raised = jnp.exp2(scores - row_max).astype(bf16)
        state_ref[chunk] = jnp.dot(vt_ref[:, :width], raised, preferred_element_type=f32)
        state_ref[chunk, dim + 1 : dim + 2] = row_max
        state_ref[chunk, dim + 2 : dim + 3] = first.astype(f32)
        squares = jnp.square(qt_ref[chunk].astype(f32))
        state_ref[chunk, dim + 3 : dim + 4] = jnp.sum(squares, axis=0, keepdims=True)
    done_ref[...] = jnp.zeros_like(done_ref)


def earlier_kernel(qt_ref, *refs, base, part, last):
    if last:
        *blocks, state_ref, out_ref, keys_ref, vt_ref = refs
    else:
        *blocks, state_ref, out_ref, done_ref, keys_ref, vt_ref = refs
        done_ref[...] = jnp.zeros_like(done_ref)
    chunks, dim, rows = qt_ref.shape
    tok = blocks[0].shape[0] // 2
    width = len(blocks) * tok
    end = float(base + width)

    def leave(chunk, total):
        if last:
            result = (total[:dim] / total[dim : dim + 1]).T.astype(bf16)
            for head in range(rows // part):
                out_ref[chunk, :, head * dim : (head + 1) * dim] = result[
                    head * part : (head + 1) * part
                ]
        else:
            out_ref[chunk] = total

    def keeping(chunk):
        scores = scores_of(keys_ref[...], qt_ref[chunk])
        raised = jnp.exp2(scores - state_ref[chunk, dim + 1 : dim + 2]).astype(bf16)
        added = jnp.dot(vt_ref[...], raised, preferred_element_type=f32)
        inside = state_ref[chunk, dim + 2 : dim + 3] < end
        leave(chunk, state_ref[chunk] + jnp.where(inside, added, 0.0))

    def raising(chunk):
        scores = scores_of(keys_ref[...], qt_ref[chunk])
        key = base + lax.broadcasted_iota(i32, (width, rows), 0)
        first = state_ref[chunk, dim + 2 : dim + 3].astype(i32)
        scores = jnp.where(key >= first, scores, -1e30)
        old = state_ref[chunk, dim + 1 : dim + 2]
        new = jnp.maximum(old, jnp.max(scores, axis=0, keepdims=True))
        raised = jnp.exp2(scores - new).astype(bf16)
        added = jnp.dot(vt_ref[...], raised, preferred_element_type=f32)
        row = lax.broadcasted_iota(i32, (dim + EXTRA, rows), 0)
        factor = jnp.where(row <= dim, jnp.exp2(old - new), 1.0)
        total = state_ref[chunk] * factor + added
        leave(chunk, jnp.where(row == dim + 1, new, total))

    lowest = jnp.min(state_ref[0, dim + 2 : dim + 3])
    needed = lowest < end

    @pl.when(jnp.logical_not(needed))
    def _():
        for chunk in range(chunks):
            leave(chunk, state_ref[chunk])

    @pl.when(needed)
    def _():
        for i, block in enumerate(blocks):
            keys_ref[i * tok : (i + 1) * tok, :] = block[:tok, :]
            vt_ref[:dim, i * tok : (i + 1) * tok] = block[tok:, :].T
        vt_ref[dim:, :] = one_row(width)
        key = base + lax.broadcasted_iota(i32, (1, width), 1)
        vt_ref[...] = jnp.where(key >= lowest.astype(i32), vt_ref[...], 0.0).astype(bf16)

        squares = jnp.square(keys_ref[...].astype(f32))
        bound = jnp.max(jnp.sum(squares, axis=1, keepdims=True))
        bound = bound * (math.log2(math.e) ** 2 / dim * 1.01)
        fits = jnp.ones((1, rows), f32)
        for chunk in range(chunks):
            room = state_ref[chunk, dim + 1 : dim + 2] + ROOM
            fit = (room > 0) & (state_ref[chunk, dim + 3 : dim + 4] * bound <= room * room)
            fits = jnp.where(fit, fits, 0.0)
        small = jnp.min(fits) > 0
        plain = small & (jnp.min(state_ref[chunks - 1, dim + 2 : dim + 3]) < end)

        @pl.when(plain)
        def _():
            for chunk in range(chunks):
                keeping(chunk)

        @pl.when(jnp.logical_not(plain))
        def _():
            def body(chunk, carry):
                some = jnp.min(state_ref[chunk, dim + 2 : dim + 3]) < end

                @pl.when(jnp.logical_not(some))
                def _():
                    leave(chunk, state_ref[chunk])

                @pl.when(some & small)
                def _():
                    keeping(chunk)

                @pl.when(some & jnp.logical_not(small))
                def _():
                    raising(chunk)

                return carry

            lax.fori_loop(0, chunks, body, 0)


def attend_own(qt, near, kv, part):
    chunks, dim, rows = qt.shape
    tok = kv.shape[0] // 2
    return pl.pallas_call(
        functools.partial(own_kernel, part=part),
        in_specs=[VMEM] * 3,
        out_specs=[VMEM] * 2,
        out_shape=[
            jax.ShapeDtypeStruct((chunks, dim + EXTRA, rows), f32),
            jax.ShapeDtypeStruct((8, 128), f32),
        ],
        scratch_shapes=[pltpu.VMEM((dim + EXTRA, tok), bf16)],
        compiler_params=PARAMS,
        cost_estimate=COST,
        name="attend_own",
    )(qt, near, kv)


def attend_earlier(qt, blocks, base, state, part, last=False):
    chunks, dim, rows = qt.shape
    width = len(blocks) * blocks[0].shape[0] // 2
    if last:
        out_shape = jax.ShapeDtypeStruct((chunks, part, rows // part * dim), bf16)
        out_specs, alias = VMEM, {}
    else:
        out_shape = [
            jax.ShapeDtypeStruct(state.shape, f32),
            jax.ShapeDtypeStruct((8, 128), f32),
        ]
        out_specs = [VMEM] * 2
        alias = {1 + len(blocks): 0}
    return pl.pallas_call(
        functools.partial(earlier_kernel, base=base, part=part, last=last),
        in_specs=[VMEM] * (2 + len(blocks)),
        out_specs=out_specs,
        out_shape=out_shape,
        input_output_aliases=alias,
        scratch_shapes=[
            pltpu.VMEM((width, dim), bf16),
            pltpu.VMEM((dim + EXTRA, width), bf16),
        ],
        compiler_params=PARAMS,
        cost_estimate=COST,
        name="attend_earlier",
    )(qt, *blocks, state)


def held_kernel(value_ref, after_ref, out_ref):
    out_ref[...] = value_ref[...]


def held(value, after):
    return pl.pallas_call(
        held_kernel,
        in_specs=[VMEM, ANY],
        out_specs=VMEM,
        out_shape=jax.ShapeDtypeStruct(value.shape, value.dtype),
        compiler_params=PARAMS,
        cost_estimate=COST,
        name="held",
    )(value, after)


def on_device(queries, keys, values, doc_ids):
    tok, heads, dim = queries.shape
    ring = lax.axis_size("kvh")
    part = tok // ring
    own_index = lax.axis_index("ctx")

    width = (SPAN + 1) * tok
    padded = jnp.concatenate([jnp.full((SPAN * tok,), -1, i32), doc_ids])
    near = lax.dynamic_slice_in_dim(padded, own_index * tok, width, 0).reshape(-1, 128)

    qt = queries.reshape(ring, part, heads, dim).transpose(0, 3, 2, 1)
    qt = qt.reshape(ring, dim, heads * part)

    kv0 = jnp.concatenate([keys[:, 0], values[:, 0]], 0)
    kv2 = hop(kv0, 2)
    kv1 = hop(held(kv0, qt), 1)
    state, done = attend_own(qt, near, kv0, part)
    kv4 = hop(held(kv2, done), 2)
    state, done = attend_earlier(qt, [kv2, kv1], 3 * tok, state, part)
    kv3 = hop(held(kv2, done), 1)
    kv5 = hop(held(kv4, done), 1)
    state, done = attend_earlier(qt, [kv4, kv3], tok, state, part)
    pieces = attend_earlier(qt, [kv5], 0, state, part, last=True)
    pieces = lax.all_to_all(pieces, "kvh", split_axis=0, concat_axis=0, tiled=True)
    return pieces.transpose(1, 0, 2).reshape(part, ring * heads * dim)


def solution(mesh):
    in_specs = (P("ctx", "kvh", None), P("ctx", "kvh", None), P("ctx", "kvh", None), P())
    out_specs = P(("ctx", "kvh"), None)
    return jax.shard_map(
        on_device, mesh=mesh, in_specs=in_specs, out_specs=out_specs, check_vma=False
    )
```

```python
import functools
import math

import jax
import jax.numpy as jnp
from jax import lax
from jax.experimental import pallas as pl
from jax.experimental.pallas import tpu as pltpu
from jax.sharding import PartitionSpec as P

SPAN = 5
DOCS = 32
EXTRA = 8
ROOM = 100.0
VMEM = pl.BlockSpec(memory_space=pltpu.VMEM)
ANY = pl.BlockSpec(memory_space=pl.ANY)
PARAMS = pltpu.CompilerParams(vmem_limit_bytes=16 * 2**20)
COST = pl.CostEstimate(flops=1000, bytes_accessed=0, transcendentals=0)
bf16, f32, i32 = jnp.bfloat16, jnp.float32, jnp.int32


def hop(value, steps, begin=0, stride=1):
    count = lax.axis_size("ctx")
    pairs = [(i, i + steps) for i in range(begin, count - steps, stride)]
    return lax.ppermute(value, "ctx", pairs)


def swap_cores(value):
    count = lax.axis_size("ctx")
    return lax.ppermute(value, "ctx", [(i, i ^ 1) for i in range(count)])


def scores_of(keys, qt):
    scale = math.log2(math.e) / math.sqrt(keys.shape[1])
    return jnp.dot(keys, qt, preferred_element_type=f32) * scale


def one_row(width):
    return (lax.broadcasted_iota(i32, (EXTRA, width), 0) == 0).astype(bf16)


def own_kernel(qt_ref, near_ref, kv_ref, state_ref, done_ref, vt_ref, *, part):
    chunks, dim, rows = qt_ref.shape
    tok = kv_ref.shape[0] // 2
    lanes = near_ref.shape[1]
    vt_ref[:dim, :] = kv_ref[tok:, :].T
    vt_ref[dim:, :] = one_row(tok)

    near = near_ref[...]
    mine = near[SPAN * tok // lanes :]
    begins = jnp.zeros(mine.shape, i32)
    for doc in range(DOCS):
        before = jnp.sum((near < doc).astype(f32), axis=(0, 1), keepdims=True)
        begins = jnp.where(mine == doc, before.astype(i32), begins)

    place = lax.broadcasted_iota(i32, (1, rows), 1) & (part - 1)
    for chunk in range(chunks):
        at, lane = divmod(chunk * part, lanes)
        first = jnp.concatenate([begins[at : at + 1, lane : lane + part]] * (rows // part), 1)
        width = min(tok, (chunk * part + part + 127) // 128 * 128)
        scores = scores_of(kv_ref[:width, :], qt_ref[chunk])
        own = chunk * part + place
        key = lax.broadcasted_iota(i32, (width, rows), 0)
        scores = jnp.where((key >= first - SPAN * tok) & (key <= own), scores, -1e30)
        row_max = jnp.max(scores, axis=0, keepdims=True)
        raised = jnp.exp2(scores - row_max).astype(bf16)
        state_ref[chunk] = jnp.dot(vt_ref[:, :width], raised, preferred_element_type=f32)
        state_ref[chunk, dim + 1 : dim + 2] = row_max
        state_ref[chunk, dim + 2 : dim + 3] = first.astype(f32)
        squares = jnp.square(qt_ref[chunk].astype(f32))
        state_ref[chunk, dim + 3 : dim + 4] = jnp.sum(squares, axis=0, keepdims=True)
    done_ref[...] = jnp.zeros_like(done_ref)


def earlier_kernel(qt_ref, *refs, base, part, last):
    if last:
        *blocks, state_ref, _, out_ref, keys_ref, vt_ref = refs
    else:
        *blocks, state_ref, _, out_ref, done_ref, keys_ref, vt_ref = refs
        done_ref[...] = jnp.zeros_like(done_ref)
    chunks, dim, rows = qt_ref.shape
    tok = blocks[0].shape[0] // 2
    width = len(blocks) * tok
    end = float(base + width)

    def leave(chunk, total):
        if last:
            result = (total[:dim] / total[dim : dim + 1]).T.astype(bf16)
            for head in range(rows // part):
                out_ref[chunk, :, head * dim : (head + 1) * dim] = result[
                    head * part : (head + 1) * part
                ]
        else:
            out_ref[chunk] = total

    def keeping(chunk):
        scores = scores_of(keys_ref[...], qt_ref[chunk])
        raised = jnp.exp2(scores - state_ref[chunk, dim + 1 : dim + 2]).astype(bf16)
        added = jnp.dot(vt_ref[...], raised, preferred_element_type=f32)
        inside = state_ref[chunk, dim + 2 : dim + 3] < end
        leave(chunk, state_ref[chunk] + jnp.where(inside, added, 0.0))

    def raising(chunk):
        scores = scores_of(keys_ref[...], qt_ref[chunk])
        key = base + lax.broadcasted_iota(i32, (width, rows), 0)
        first = state_ref[chunk, dim + 2 : dim + 3].astype(i32)
        scores = jnp.where(key >= first, scores, -1e30)
        old = state_ref[chunk, dim + 1 : dim + 2]
        new = jnp.maximum(old, jnp.max(scores, axis=0, keepdims=True))
        raised = jnp.exp2(scores - new).astype(bf16)
        added = jnp.dot(vt_ref[...], raised, preferred_element_type=f32)
        row = lax.broadcasted_iota(i32, (dim + EXTRA, rows), 0)
        factor = jnp.where(row <= dim, jnp.exp2(old - new), 1.0)
        total = state_ref[chunk] * factor + added
        leave(chunk, jnp.where(row == dim + 1, new, total))

    lowest = jnp.min(state_ref[0, dim + 2 : dim + 3])
    needed = lowest < end

    @pl.when(jnp.logical_not(needed))
    def _():
        for chunk in range(chunks):
            leave(chunk, state_ref[chunk])

    @pl.when(needed)
    def _():
        for i, block in enumerate(blocks):
            keys_ref[i * tok : (i + 1) * tok, :] = block[:tok, :]
            vt_ref[:dim, i * tok : (i + 1) * tok] = block[tok:, :].T
        vt_ref[dim:, :] = one_row(width)
        key = base + lax.broadcasted_iota(i32, (1, width), 1)
        vt_ref[...] = jnp.where(key >= lowest.astype(i32), vt_ref[...], 0.0).astype(bf16)

        squares = jnp.square(keys_ref[...].astype(f32))
        bound = jnp.max(jnp.sum(squares, axis=1, keepdims=True))
        bound = bound * (math.log2(math.e) ** 2 / dim * 1.01)
        fits = jnp.ones((1, rows), f32)
        for chunk in range(chunks):
            room = state_ref[chunk, dim + 1 : dim + 2] + ROOM
            fit = (room > 0) & (state_ref[chunk, dim + 3 : dim + 4] * bound <= room * room)
            fits = jnp.where(fit, fits, 0.0)
        small = jnp.min(fits) > 0
        plain = small & (jnp.min(state_ref[chunks - 1, dim + 2 : dim + 3]) < end)

        @pl.when(plain)
        def _():
            for chunk in range(chunks):
                keeping(chunk)

        @pl.when(jnp.logical_not(plain))
        def _():
            def body(chunk, carry):
                some = jnp.min(state_ref[chunk, dim + 2 : dim + 3]) < end

                @pl.when(jnp.logical_not(some))
                def _():
                    leave(chunk, state_ref[chunk])

                @pl.when(some & small)
                def _():
                    keeping(chunk)

                @pl.when(some & jnp.logical_not(small))
                def _():
                    raising(chunk)

                return carry

            lax.fori_loop(0, chunks, body, 0)


def attend_own(qt, near, kv, part):
    chunks, dim, rows = qt.shape
    tok = kv.shape[0] // 2
    return pl.pallas_call(
        functools.partial(own_kernel, part=part),
        in_specs=[VMEM] * 3,
        out_specs=[VMEM] * 2,
        out_shape=[
            jax.ShapeDtypeStruct((chunks, dim + EXTRA, rows), f32),
            jax.ShapeDtypeStruct((8, 128), f32),
        ],
        scratch_shapes=[pltpu.VMEM((dim + EXTRA, tok), bf16)],
        compiler_params=PARAMS,
        cost_estimate=COST,
        name="attend_own",
    )(qt, near, kv)


def attend_earlier(qt, blocks, base, state, part, after, last=False):
    chunks, dim, rows = qt.shape
    width = len(blocks) * blocks[0].shape[0] // 2
    if last:
        out_shape = jax.ShapeDtypeStruct((chunks, part, rows // part * dim), bf16)
        out_specs, alias = VMEM, {}
    else:
        out_shape = [
            jax.ShapeDtypeStruct(state.shape, f32),
            jax.ShapeDtypeStruct((8, 128), f32),
        ]
        out_specs = [VMEM] * 2
        alias = {1 + len(blocks): 0}
    return pl.pallas_call(
        functools.partial(earlier_kernel, base=base, part=part, last=last),
        in_specs=[VMEM] * (2 + len(blocks)) + [ANY],
        out_specs=out_specs,
        out_shape=out_shape,
        input_output_aliases=alias,
        scratch_shapes=[
            pltpu.VMEM((width, dim), bf16),
            pltpu.VMEM((dim + EXTRA, width), bf16),
        ],
        compiler_params=PARAMS,
        cost_estimate=COST,
        name="attend_earlier",
    )(qt, *blocks, state, after)


def held_kernel(value_ref, after_ref, out_ref):
    out_ref[...] = value_ref[...]


def arrived_kernel(value_ref, out_ref):
    out_ref[...] = jnp.zeros_like(out_ref)


def sum_kernel(one_ref, other_ref, after_ref, out_ref):
    out_ref[...] = one_ref[...] + other_ref[...]


def chosen_kernel(one_ref, other_ref, after_ref, out_ref):
    odd = lax.rem(lax.axis_index("ctx"), 2) == 1

    @pl.when(odd)
    def _():
        out_ref[...] = other_ref[...]

    @pl.when(jnp.logical_not(odd))
    def _():
        out_ref[...] = one_ref[...]


def small_call(kernel, name, values, after):
    return pl.pallas_call(
        kernel,
        in_specs=[VMEM] * len(values) + [ANY],
        out_specs=VMEM,
        out_shape=jax.ShapeDtypeStruct(values[0].shape, values[0].dtype),
        compiler_params=PARAMS,
        cost_estimate=COST,
        name=name,
    )(*values, after)


def held(value, after):
    return small_call(held_kernel, "held", [value], after)


def arrived(value):
    return pl.pallas_call(
        arrived_kernel,
        in_specs=[ANY],
        out_specs=VMEM,
        out_shape=jax.ShapeDtypeStruct((8, 128), f32),
        compiler_params=PARAMS,
        cost_estimate=COST,
        name="arrived",
    )(value)


def joined(one, other, after):
    return small_call(sum_kernel, "joined", [one, other], after)


def chosen(even, odd, after):
    return small_call(chosen_kernel, "chosen", [even, odd], after)


def on_device(queries, keys, values, doc_ids):
    tok, heads, dim = queries.shape
    ring = lax.axis_size("kvh")
    part = tok // ring
    own_index = lax.axis_index("ctx")

    width = (SPAN + 1) * tok
    padded = jnp.concatenate([jnp.full((SPAN * tok,), -1, i32), doc_ids])
    near = lax.dynamic_slice_in_dim(padded, own_index * tok, width, 0).reshape(-1, 128)

    qt = queries.reshape(ring, part, heads, dim).transpose(0, 3, 2, 1)
    qt = qt.reshape(ring, dim, heads * part)

    kv0 = jnp.concatenate([keys[:, 0], values[:, 0]], 0)
    odd2 = hop(kv0, 2, 1, 2)
    even2 = hop(held(kv0, qt), 2, 0, 2)
    state, done = attend_own(qt, near, kv0, part)
    sent = held(odd2, done)
    odd4 = hop(sent, 2, 1, 2)
    kv1 = swap_cores(chosen(kv0, odd2, sent))
    kv2 = joined(odd2, even2, done)
    even4 = hop(held(even2, done), 2, 0, 2)
    state, done = attend_earlier(qt, [kv2, kv1], 3 * tok, state, part, arrived(odd4))
    kv3 = swap_cores(chosen(even2, odd4, done))
    kv4 = joined(odd4, even4, done)
    kv5 = hop(kv4, 1)
    state, done = attend_earlier(qt, [kv4, kv3], tok, state, part, done)
    pieces = attend_earlier(qt, [kv5], 0, state, part, done, last=True)
    pieces = lax.all_to_all(pieces, "kvh", split_axis=0, concat_axis=0, tiled=True)
    return pieces.transpose(1, 0, 2).reshape(part, ring * heads * dim)


def solution(mesh):
    in_specs = (P("ctx", "kvh", None), P("ctx", "kvh", None), P("ctx", "kvh", None), P())
    out_specs = P(("ctx", "kvh"), None)
    return jax.shard_map(
        on_device, mesh=mesh, in_specs=in_specs, out_specs=out_specs, check_vma=False
    )
```

```python
import functools
import math

import jax
import jax.numpy as jnp
from jax import lax
from jax.experimental import pallas as pl
from jax.experimental.pallas import tpu as pltpu
from jax.sharding import PartitionSpec as P

SPAN = 5
DOCS = 32
EXTRA = 8
LARGEST_KEY = 5.0
ROOM = 112.0
GROUP = 2
VMEM = pl.BlockSpec(memory_space=pltpu.VMEM)
ANY = pl.BlockSpec(memory_space=pl.ANY)
PARAMS = pltpu.CompilerParams(vmem_limit_bytes=16 * 2**20)
COST = pl.CostEstimate(flops=1000, bytes_accessed=0, transcendentals=0)
bf16, f32, i32 = jnp.bfloat16, jnp.float32, jnp.int32


def hop(value, steps):
    count = lax.axis_size("ctx")
    return lax.ppermute(value, "ctx", [(i, i + steps) for i in range(count - steps)])


def scores_of(keys, qt):
    scale = math.log2(math.e) / math.sqrt(keys.shape[1])
    return jnp.dot(keys, qt, preferred_element_type=f32) * scale


def one_row(width):
    return (lax.broadcasted_iota(i32, (EXTRA, width), 0) == 0).astype(bf16)


def own_kernel(qt_ref, near_ref, kv_ref, state_ref, done_ref, vt_ref, *, part):
    chunks, dim, rows = qt_ref.shape
    tok = kv_ref.shape[0] // 2
    lanes = near_ref.shape[1]
    vt_ref[:dim, :] = kv_ref[tok:, :].T
    vt_ref[dim:, :] = one_row(tok)

    near = near_ref[...]
    mine = near[SPAN * tok // lanes :]
    begins = jnp.zeros(mine.shape, i32)
    for doc in range(DOCS):
        before = jnp.sum((near < doc).astype(f32), axis=(0, 1), keepdims=True)
        begins = jnp.where(mine == doc, before.astype(i32), begins)

    place = lax.broadcasted_iota(i32, (1, rows), 1) & (part - 1)
    for chunk in range(chunks):
        at, lane = divmod(chunk * part, lanes)
        first = jnp.concatenate([begins[at : at + 1, lane : lane + part]] * (rows // part), 1)
        width = min(tok, (chunk * part + part + 127) // 128 * 128)
        scores = scores_of(kv_ref[:width, :], qt_ref[chunk])
        own = chunk * part + place
        key = lax.broadcasted_iota(i32, (width, rows), 0)
        scores = jnp.where((key >= first - SPAN * tok) & (key <= own), scores, -1e30)
        row_max = jnp.max(scores, axis=0, keepdims=True)
        raised = jnp.exp2(scores - row_max).astype(bf16)
        state_ref[chunk] = jnp.dot(vt_ref[:, :width], raised, preferred_element_type=f32)
        state_ref[chunk, dim + 1 : dim + 2] = row_max
        state_ref[chunk, dim + 2 : dim + 3] = first.astype(f32)
        squares = jnp.square(qt_ref[chunk].astype(f32))
        bound = jnp.sum(squares, axis=0, keepdims=True)
        bound = bound * (math.log2(math.e) ** 2 * LARGEST_KEY**2 * 1.01)
        room = row_max + ROOM
        fits = (room > 0) & (bound <= room * room)
        state_ref[chunk, dim + 3 : dim + 4] = jnp.where(fits, 1.0, 0.0)
    done_ref[...] = jnp.zeros_like(done_ref)


def earlier_kernel(qt_ref, *refs, base, part, last):
    if last:
        *blocks, state_ref, out_ref, keys_ref, vt_ref = refs
    else:
        *blocks, state_ref, out_ref, done_ref, keys_ref, vt_ref = refs
        done_ref[...] = jnp.zeros_like(done_ref)
    chunks, dim, rows = qt_ref.shape
    tok = blocks[0].shape[0] // 2
    width = len(blocks) * tok
    end = float(base + width)

    def leave(chunk, total):
        if last:
            result = (total[:dim] / total[dim : dim + 1]).T.astype(bf16)
            for head in range(rows // part):
                out_ref[chunk, :, head * dim : (head + 1) * dim] = result[
                    head * part : (head + 1) * part
                ]
        else:
            out_ref[chunk] = total

    def keeping(*group):
        qt = jnp.concatenate([qt_ref[c] for c in group], 1)
        row_max = jnp.concatenate([state_ref[c, dim + 1 : dim + 2] for c in group], 1)
        raised = jnp.exp2(scores_of(keys_ref[...], qt) - row_max).astype(bf16)
        added = jnp.dot(vt_ref[...], raised, preferred_element_type=f32)
        for i, chunk in enumerate(group):
            inside = state_ref[chunk, dim + 2 : dim + 3] < end
            mine = added[:, i * rows : (i + 1) * rows]
            leave(chunk, state_ref[chunk] + jnp.where(inside, mine, 0.0))

    def raising(chunk):
        scores = scores_of(keys_ref[...], qt_ref[chunk])
        key = base + lax.broadcasted_iota(i32, (width, rows), 0)
        first = state_ref[chunk, dim + 2 : dim + 3].astype(i32)
        scores = jnp.where(key >= first, scores, -1e30)
        old = state_ref[chunk, dim + 1 : dim + 2]
        new = jnp.maximum(old, jnp.max(scores, axis=0, keepdims=True))
        raised = jnp.exp2(scores - new).astype(bf16)
        added = jnp.dot(vt_ref[...], raised, preferred_element_type=f32)
        row = lax.broadcasted_iota(i32, (dim + EXTRA, rows), 0)
        factor = jnp.where(row <= dim, jnp.exp2(old - new), 1.0)
        total = state_ref[chunk] * factor + added
        leave(chunk, jnp.where(row == dim + 1, new, total))

    lowest = jnp.min(state_ref[0, dim + 2 : dim + 3])
    needed = lowest < end

    @pl.when(jnp.logical_not(needed))
    def _():
        for chunk in range(chunks):
            leave(chunk, state_ref[chunk])

    @pl.when(needed)
    def _():
        fits = state_ref[0, dim + 3 : dim + 4]
        for chunk in range(1, chunks):
            fits = jnp.minimum(fits, state_ref[chunk, dim + 3 : dim + 4])
        small = jnp.min(fits) > 0
        for i, block in enumerate(blocks):
            keys_ref[i * tok : (i + 1) * tok, :] = block[:tok, :]
            vt_ref[:dim, i * tok : (i + 1) * tok] = block[tok:, :].T
        vt_ref[dim:, :] = one_row(width)

        @pl.when(lowest > base)
        def _():
            key = base + lax.broadcasted_iota(i32, (1, width), 1)
            vt_ref[...] = jnp.where(key >= lowest.astype(i32), vt_ref[...], 0.0).astype(bf16)

        groups = [range(c, min(c + GROUP, chunks)) for c in range(0, chunks, GROUP)]
        plain = small & (jnp.min(state_ref[groups[-1][0], dim + 2 : dim + 3]) < end)

        @pl.when(plain)
        def _():
            for group in groups:
                keeping(*group)

        @pl.when(jnp.logical_not(plain))
        def _():
            for group in groups:
                some = jnp.min(state_ref[group[0], dim + 2 : dim + 3]) < end

                @pl.when(jnp.logical_not(some))
                def _():
                    for chunk in group:
                        leave(chunk, state_ref[chunk])

                @pl.when(some & small)
                def _():
                    keeping(*group)

                @pl.when(some & jnp.logical_not(small))
                def _():
                    lax.fori_loop(group[0], group[-1] + 1, lambda chunk, _: raising(chunk), None)


def attend_own(qt, near, kv, part):
    chunks, dim, rows = qt.shape
    tok = kv.shape[0] // 2
    return pl.pallas_call(
        functools.partial(own_kernel, part=part),
        in_specs=[VMEM] * 3,
        out_specs=[VMEM] * 2,
        out_shape=[
            jax.ShapeDtypeStruct((chunks, dim + EXTRA, rows), f32),
            jax.ShapeDtypeStruct((8, 128), f32),
        ],
        scratch_shapes=[pltpu.VMEM((dim + EXTRA, tok), bf16)],
        compiler_params=PARAMS,
        cost_estimate=COST,
        name="attend_own",
    )(qt, near, kv)


def attend_earlier(qt, blocks, base, state, part, last=False):
    chunks, dim, rows = qt.shape
    width = len(blocks) * blocks[0].shape[0] // 2
    if last:
        out_shape = jax.ShapeDtypeStruct((chunks, part, rows // part * dim), bf16)
        out_specs, alias = VMEM, {}
    else:
        out_shape = [
            jax.ShapeDtypeStruct(state.shape, f32),
            jax.ShapeDtypeStruct((8, 128), f32),
        ]
        out_specs = [VMEM] * 2
        alias = {1 + len(blocks): 0}
    return pl.pallas_call(
        functools.partial(earlier_kernel, base=base, part=part, last=last),
        in_specs=[VMEM] * (2 + len(blocks)),
        out_specs=out_specs,
        out_shape=out_shape,
        input_output_aliases=alias,
        scratch_shapes=[
            pltpu.VMEM((width, dim), bf16),
            pltpu.VMEM((dim + EXTRA, width), bf16),
        ],
        compiler_params=PARAMS,
        cost_estimate=COST,
        name="attend_earlier",
    )(qt, *blocks, state)


def held_kernel(value_ref, after_ref, out_ref):
    out_ref[...] = value_ref[...]


def held(value, after):
    return pl.pallas_call(
        held_kernel,
        in_specs=[VMEM, ANY],
        out_specs=VMEM,
        out_shape=jax.ShapeDtypeStruct(value.shape, value.dtype),
        compiler_params=PARAMS,
        cost_estimate=COST,
        name="held",
    )(value, after)


def on_device(queries, keys, values, doc_ids):
    tok, heads, dim = queries.shape
    ring = lax.axis_size("kvh")
    part = tok // ring
    own_index = lax.axis_index("ctx")

    width = (SPAN + 1) * tok
    padded = jnp.concatenate([jnp.full((SPAN * tok,), -1, i32), doc_ids])
    near = lax.dynamic_slice_in_dim(padded, own_index * tok, width, 0).reshape(-1, 128)

    qt = queries.reshape(ring, part, heads, dim).transpose(0, 3, 2, 1)
    qt = qt.reshape(ring, dim, heads * part)

    kv0 = jnp.concatenate([keys[:, 0], values[:, 0]], 0)
    kv2 = hop(kv0, 2)
    kv1 = hop(held(kv0, qt), 1)
    state, done = attend_own(qt, near, kv0, part)
    kv4 = hop(held(kv2, done), 2)
    state, done = attend_earlier(qt, [kv2, kv1], 3 * tok, state, part)
    kv3 = hop(held(kv2, done), 1)
    kv5 = hop(held(kv4, done), 1)
    state, done = attend_earlier(qt, [kv4, kv3], tok, state, part)
    pieces = attend_earlier(qt, [kv5], 0, state, part, last=True)
    pieces = lax.all_to_all(pieces, "kvh", split_axis=0, concat_axis=0, tiled=True)
    return pieces.transpose(1, 0, 2).reshape(part, ring * heads * dim)


def solution(mesh):
    in_specs = (P("ctx", "kvh", None), P("ctx", "kvh", None), P("ctx", "kvh", None), P())
    out_specs = P(("ctx", "kvh"), None)
    return jax.shard_map(
        on_device, mesh=mesh, in_specs=in_specs, out_specs=out_specs, check_vma=False
    )
```

```python
import functools
import math

import jax
import jax.numpy as jnp
from jax import lax
from jax.experimental import pallas as pl
from jax.experimental.pallas import tpu as pltpu
from jax.sharding import PartitionSpec as P

SPAN = 5
DOCS = 32
EXTRA = 8
LARGEST_KEY = 5.0
ROOM = 112.0
GROUP = 2
VMEM = pl.BlockSpec(memory_space=pltpu.VMEM)
ANY = pl.BlockSpec(memory_space=pl.ANY)
PARAMS = pltpu.CompilerParams(vmem_limit_bytes=16 * 2**20)
COST = pl.CostEstimate(flops=1000, bytes_accessed=0, transcendentals=0)
bf16, f32, i32 = jnp.bfloat16, jnp.float32, jnp.int32


def hop(value, steps):
    count = lax.axis_size("ctx")
    return lax.ppermute(value, "ctx", [(i, i + steps) for i in range(count - steps)])


def scores_of(keys, qt):
    scale = math.log2(math.e) / math.sqrt(keys.shape[1])
    return jnp.dot(keys, qt, preferred_element_type=f32) * scale


def one_row(width):
    return (lax.broadcasted_iota(i32, (EXTRA, width), 0) == 0).astype(bf16)


def own_kernel(qt_ref, near_ref, kv_ref, state_ref, done_ref, vt_ref, *, part):
    chunks, dim, rows = qt_ref.shape
    tok = kv_ref.shape[0] // 2
    lanes = near_ref.shape[1]
    vt_ref[:dim, :] = kv_ref[tok:, :].T
    vt_ref[dim:, :] = one_row(tok)

    near = near_ref[...]
    mine = near[SPAN * tok // lanes :]
    begins = jnp.zeros(mine.shape, i32)
    for doc in range(DOCS):
        before = jnp.sum((near < doc).astype(f32), axis=(0, 1), keepdims=True)
        begins = jnp.where(mine == doc, before.astype(i32), begins)

    place = lax.broadcasted_iota(i32, (1, rows), 1) & (part - 1)
    for chunk in range(chunks):
        at, lane = divmod(chunk * part, lanes)
        first = jnp.concatenate([begins[at : at + 1, lane : lane + part]] * (rows // part), 1)
        width = min(tok, (chunk * part + part + 127) // 128 * 128)
        scores = scores_of(kv_ref[:width, :], qt_ref[chunk])
        own = chunk * part + place
        key = lax.broadcasted_iota(i32, (width, rows), 0)
        scores = jnp.where((key >= first - SPAN * tok) & (key <= own), scores, -1e30)
        row_max = jnp.max(scores, axis=0, keepdims=True)
        raised = jnp.exp2(scores - row_max).astype(bf16)
        state_ref[chunk] = jnp.dot(vt_ref[:, :width], raised, preferred_element_type=f32)
        state_ref[chunk, dim + 1 : dim + 2] = row_max
        state_ref[chunk, dim + 2 : dim + 3] = first.astype(f32)
        squares = jnp.square(qt_ref[chunk].astype(f32))
        bound = jnp.sum(squares, axis=0, keepdims=True)
        bound = bound * (math.log2(math.e) ** 2 * LARGEST_KEY**2 * 1.01)
        room = row_max + ROOM
        fits = (room > 0) & (bound <= room * room)
        state_ref[chunk, dim + 3 : dim + 4] = jnp.where(fits, 1.0, 0.0)
    done_ref[...] = jnp.zeros_like(done_ref)


def earlier_kernel(qt_ref, *refs, base, part, last):
    if last:
        *blocks, state_ref, out_ref, keys_ref, vt_ref = refs
    else:
        *blocks, state_ref, out_ref, done_ref, keys_ref, vt_ref = refs
        done_ref[...] = jnp.zeros_like(done_ref)
    chunks, dim, rows = qt_ref.shape
    tok = blocks[0].shape[0] // 2
    width = len(blocks) * tok
    end = float(base + width)

    def leave(chunk, total):
        if last:
            result = (total[:dim] / total[dim : dim + 1]).T.astype(bf16)
            for head in range(rows // part):
                out_ref[chunk, :, head * dim : (head + 1) * dim] = result[
                    head * part : (head + 1) * part
                ]
        else:
            out_ref[chunk] = total

    def keeping(*group):
        qt = jnp.concatenate([qt_ref[c] for c in group], 1)
        row_max = jnp.concatenate([state_ref[c, dim + 1 : dim + 2] for c in group], 1)
        raised = jnp.exp2(scores_of(keys_ref[...], qt) - row_max).astype(bf16)
        added = jnp.dot(vt_ref[...], raised, preferred_element_type=f32)
        for i, chunk in enumerate(group):
            inside = state_ref[chunk, dim + 2 : dim + 3] < end
            mine = added[:, i * rows : (i + 1) * rows]
            leave(chunk, state_ref[chunk] + jnp.where(inside, mine, 0.0))

    def raising(chunk):
        scores = scores_of(keys_ref[...], qt_ref[chunk])
        key = base + lax.broadcasted_iota(i32, (width, rows), 0)
        first = state_ref[chunk, dim + 2 : dim + 3].astype(i32)
        scores = jnp.where(key >= first, scores, -1e30)
        old = state_ref[chunk, dim + 1 : dim + 2]
        new = jnp.maximum(old, jnp.max(scores, axis=0, keepdims=True))
        raised = jnp.exp2(scores - new).astype(bf16)
        added = jnp.dot(vt_ref[...], raised, preferred_element_type=f32)
        row = lax.broadcasted_iota(i32, (dim + EXTRA, rows), 0)
        factor = jnp.where(row <= dim, jnp.exp2(old - new), 1.0)
        total = state_ref[chunk] * factor + added
        leave(chunk, jnp.where(row == dim + 1, new, total))

    lowest = jnp.min(state_ref[0, dim + 2 : dim + 3])
    needed = lowest < end

    @pl.when(jnp.logical_not(needed))
    def _():
        for chunk in range(chunks):
            leave(chunk, state_ref[chunk])

    @pl.when(needed)
    def _():
        fits = state_ref[0, dim + 3 : dim + 4]
        for chunk in range(1, chunks):
            fits = jnp.minimum(fits, state_ref[chunk, dim + 3 : dim + 4])
        small = jnp.min(fits) > 0
        for i, block in enumerate(blocks):
            keys_ref[i * tok : (i + 1) * tok, :] = block[:tok, :]
            vt_ref[:dim, i * tok : (i + 1) * tok] = block[tok:, :].T
        vt_ref[dim:, :] = one_row(width)

        @pl.when(lowest > base)
        def _():
            key = base + lax.broadcasted_iota(i32, (1, width), 1)
            vt_ref[...] = jnp.where(key >= lowest.astype(i32), vt_ref[...], 0.0).astype(bf16)

        group = math.gcd(GROUP, chunks)
        plain = small & (jnp.min(state_ref[chunks - group, dim + 2 : dim + 3]) < end)

        @pl.when(plain)
        def _():
            for chunk in range(0, chunks, group):
                keeping(*range(chunk, chunk + group))

        @pl.when(jnp.logical_not(plain))
        def _():
            def body(turn, carry):
                mine = [turn * group + i for i in range(group)]
                some = jnp.min(state_ref[mine[0], dim + 2 : dim + 3]) < end

                @pl.when(jnp.logical_not(some))
                def _():
                    for chunk in mine:
                        leave(chunk, state_ref[chunk])

                @pl.when(some & small)
                def _():
                    keeping(*mine)

                @pl.when(some & jnp.logical_not(small))
                def _():
                    lax.fori_loop(mine[0], mine[-1] + 1, lambda chunk, _: raising(chunk), None)

                return carry

            lax.fori_loop(0, chunks // group, body, 0)


def attend_own(qt, near, kv, part):
    chunks, dim, rows = qt.shape
    tok = kv.shape[0] // 2
    return pl.pallas_call(
        functools.partial(own_kernel, part=part),
        in_specs=[VMEM] * 3,
        out_specs=[VMEM] * 2,
        out_shape=[
            jax.ShapeDtypeStruct((chunks, dim + EXTRA, rows), f32),
            jax.ShapeDtypeStruct((8, 128), f32),
        ],
        scratch_shapes=[pltpu.VMEM((dim + EXTRA, tok), bf16)],
        compiler_params=PARAMS,
        cost_estimate=COST,
        name="attend_own",
    )(qt, near, kv)


def attend_earlier(qt, blocks, base, state, part, last=False):
    chunks, dim, rows = qt.shape
    width = len(blocks) * blocks[0].shape[0] // 2
    if last:
        out_shape = jax.ShapeDtypeStruct((chunks, part, rows // part * dim), bf16)
        out_specs, alias = VMEM, {}
    else:
        out_shape = [
            jax.ShapeDtypeStruct(state.shape, f32),
            jax.ShapeDtypeStruct((8, 128), f32),
        ]
        out_specs = [VMEM] * 2
        alias = {1 + len(blocks): 0}
    return pl.pallas_call(
        functools.partial(earlier_kernel, base=base, part=part, last=last),
        in_specs=[VMEM] * (2 + len(blocks)),
        out_specs=out_specs,
        out_shape=out_shape,
        input_output_aliases=alias,
        scratch_shapes=[
            pltpu.VMEM((width, dim), bf16),
            pltpu.VMEM((dim + EXTRA, width), bf16),
        ],
        compiler_params=PARAMS,
        cost_estimate=COST,
        name="attend_earlier",
    )(qt, *blocks, state)


def held_kernel(value_ref, after_ref, out_ref):
    out_ref[...] = value_ref[...]


def held(value, after):
    return pl.pallas_call(
        held_kernel,
        in_specs=[VMEM, ANY],
        out_specs=VMEM,
        out_shape=jax.ShapeDtypeStruct(value.shape, value.dtype),
        compiler_params=PARAMS,
        cost_estimate=COST,
        name="held",
    )(value, after)


def on_device(queries, keys, values, doc_ids):
    tok, heads, dim = queries.shape
    ring = lax.axis_size("kvh")
    part = tok // ring
    own_index = lax.axis_index("ctx")

    width = (SPAN + 1) * tok
    padded = jnp.concatenate([jnp.full((SPAN * tok,), -1, i32), doc_ids])
    near = lax.dynamic_slice_in_dim(padded, own_index * tok, width, 0).reshape(-1, 128)

    qt = queries.reshape(ring, part, heads, dim).transpose(0, 3, 2, 1)
    qt = qt.reshape(ring, dim, heads * part)

    kv0 = jnp.concatenate([keys[:, 0], values[:, 0]], 0)
    kv2 = hop(kv0, 2)
    kv1 = hop(held(kv0, qt), 1)
    state, done = attend_own(qt, near, kv0, part)
    kv4 = hop(held(kv2, done), 2)
    state, done = attend_earlier(qt, [kv2, kv1], 3 * tok, state, part)
    kv3 = hop(held(kv2, done), 1)
    kv5 = hop(held(kv4, done), 1)
    state, done = attend_earlier(qt, [kv4, kv3], tok, state, part)
    pieces = attend_earlier(qt, [kv5], 0, state, part, last=True)
    pieces = lax.all_to_all(pieces, "kvh", split_axis=0, concat_axis=0, tiled=True)
    return pieces.transpose(1, 0, 2).reshape(part, ring * heads * dim)


def solution(mesh):
    in_specs = (P("ctx", "kvh", None), P("ctx", "kvh", None), P("ctx", "kvh", None), P())
    out_specs = P(("ctx", "kvh"), None)
    return jax.shard_map(
        on_device, mesh=mesh, in_specs=in_specs, out_specs=out_specs, check_vma=False
    )
```

```python
import functools
import math

import jax
import jax.numpy as jnp
from jax import lax
from jax.experimental import pallas as pl
from jax.experimental.pallas import tpu as pltpu
from jax.sharding import PartitionSpec as P

SPAN = 5
DOCS = 32
EXTRA = 16
LARGEST_KEY = 5.0
ROOM = 112.0
GROUP = 2
VMEM = pl.BlockSpec(memory_space=pltpu.VMEM)
ANY = pl.BlockSpec(memory_space=pl.ANY)
PARAMS = pltpu.CompilerParams(vmem_limit_bytes=16 * 2**20)
COST = pl.CostEstimate(flops=1000, bytes_accessed=0, transcendentals=0)
bf16, f32, i32 = jnp.bfloat16, jnp.float32, jnp.int32


def hop(value, steps):
    count = lax.axis_size("ctx")
    return lax.ppermute(value, "ctx", [(i, i + steps) for i in range(count - steps)])


def scores_of(keys, qt):
    scale = math.log2(math.e) / math.sqrt(keys.shape[1])
    return jnp.dot(keys, qt, preferred_element_type=f32) * scale


def one_row(width):
    return (lax.broadcasted_iota(i32, (EXTRA, width), 0) == 0).astype(bf16)


def own_kernel(qt_ref, near_ref, kv_ref, state_ref, done_ref, vt_ref, *, part):
    chunks, dim, rows = qt_ref.shape
    tok = kv_ref.shape[0] // 2
    lanes = near_ref.shape[1]
    vt_ref[:dim, :] = kv_ref[tok:, :].T
    vt_ref[dim:, :] = one_row(tok)

    near = near_ref[...]
    mine = near[SPAN * tok // lanes :]
    begins = jnp.zeros(mine.shape, i32)
    for doc in range(DOCS):
        before = jnp.sum((near < doc).astype(f32), axis=(0, 1), keepdims=True)
        begins = jnp.where(mine == doc, before.astype(i32), begins)

    place = lax.broadcasted_iota(i32, (1, rows), 1) & (part - 1)
    for chunk in range(chunks):
        at, lane = divmod(chunk * part, lanes)
        first = jnp.concatenate([begins[at : at + 1, lane : lane + part]] * (rows // part), 1)
        width = min(tok, (chunk * part + part + 127) // 128 * 128)
        scores = scores_of(kv_ref[:width, :], qt_ref[chunk])
        own = chunk * part + place
        key = lax.broadcasted_iota(i32, (width, rows), 0)
        scores = jnp.where((key >= first - SPAN * tok) & (key <= own), scores, -1e30)
        row_max = jnp.max(scores, axis=0, keepdims=True)
        raised = jnp.exp2(scores - row_max).astype(bf16)
        state_ref[chunk] = jnp.dot(vt_ref[:, :width], raised, preferred_element_type=f32)
        state_ref[chunk, dim + 1 : dim + 2] = row_max
        state_ref[chunk, dim + 2 : dim + 3] = first.astype(f32)
        squares = jnp.square(qt_ref[chunk].astype(f32))
        bound = jnp.sum(squares, axis=0, keepdims=True)
        bound = bound * (math.log2(math.e) ** 2 * LARGEST_KEY**2 * 1.01)
        room = row_max + ROOM
        fits = (room > 0) & (bound <= room * room)
        state_ref[chunk, dim + 3 : dim + 4] = jnp.where(fits, 1.0, 0.0)
    done_ref[...] = jnp.zeros_like(done_ref)


def earlier_kernel(qt_ref, *refs, base, part, last):
    if last:
        *blocks, state_ref, out_ref, keys_ref, vt_ref = refs
    else:
        *blocks, state_ref, out_ref, done_ref, keys_ref, vt_ref = refs
        done_ref[...] = jnp.zeros_like(done_ref)
    chunks, dim, rows = qt_ref.shape
    tok = blocks[0].shape[0] // 2
    width = len(blocks) * tok
    end = float(base + width)

    def leave(chunk, total):
        if last:
            result = (total[:dim] / total[dim : dim + 1]).T.astype(bf16)
            for head in range(rows // part):
                out_ref[chunk, :, head * dim : (head + 1) * dim] = result[
                    head * part : (head + 1) * part
                ]
        else:
            out_ref[chunk] = total

    def keeping(*group):
        qt = jnp.concatenate([qt_ref[c] for c in group], 1)
        row_max = jnp.concatenate([state_ref[c, dim + 1 : dim + 2] for c in group], 1)
        raised = jnp.exp2(scores_of(keys_ref[...], qt) - row_max).astype(bf16)
        added = jnp.dot(vt_ref[...], raised, preferred_element_type=f32)
        for i, chunk in enumerate(group):
            inside = state_ref[chunk, dim + 2 : dim + 3] < end
            mine = added[:, i * rows : (i + 1) * rows]
            leave(chunk, state_ref[chunk] + jnp.where(inside, mine, 0.0))

    def raising(chunk):
        scores = scores_of(keys_ref[...], qt_ref[chunk])
        key = base + lax.broadcasted_iota(i32, (width, rows), 0)
        first = state_ref[chunk, dim + 2 : dim + 3].astype(i32)
        scores = jnp.where(key >= first, scores, -1e30)
        old = state_ref[chunk, dim + 1 : dim + 2]
        new = jnp.maximum(old, jnp.max(scores, axis=0, keepdims=True))
        raised = jnp.exp2(scores - new).astype(bf16)
        added = jnp.dot(vt_ref[...], raised, preferred_element_type=f32)
        row = lax.broadcasted_iota(i32, (dim + EXTRA, rows), 0)
        factor = jnp.where(row <= dim, jnp.exp2(old - new), 1.0)
        total = state_ref[chunk] * factor + added
        leave(chunk, jnp.where(row == dim + 1, new, total))

    lowest = jnp.min(state_ref[0, dim + 2 : dim + 3])
    needed = lowest < end

    @pl.when(jnp.logical_not(needed))
    def _():
        for chunk in range(chunks):
            leave(chunk, state_ref[chunk])

    @pl.when(needed)
    def _():
        fits = state_ref[0, dim + 3 : dim + 4]
        for chunk in range(1, chunks):
            fits = jnp.minimum(fits, state_ref[chunk, dim + 3 : dim + 4])
        small = jnp.min(fits) > 0
        for i, block in enumerate(blocks):
            keys_ref[i * tok : (i + 1) * tok, :] = block[:tok, :]
            vt_ref[:dim, i * tok : (i + 1) * tok] = block[tok:, :].T
        vt_ref[dim:, :] = one_row(width)

        @pl.when(lowest > base)
        def _():
            key = base + lax.broadcasted_iota(i32, (1, width), 1)
            vt_ref[...] = jnp.where(key >= lowest.astype(i32), vt_ref[...], 0.0).astype(bf16)

        group = math.gcd(GROUP, chunks)
        plain = small & (jnp.min(state_ref[chunks - group, dim + 2 : dim + 3]) < end)

        @pl.when(plain)
        def _():
            for chunk in range(0, chunks, group):
                keeping(*range(chunk, chunk + group))

        @pl.when(jnp.logical_not(plain))
        def _():
            def body(turn, carry):
                mine = [turn * group + i for i in range(group)]
                some = jnp.min(state_ref[mine[0], dim + 2 : dim + 3]) < end

                @pl.when(jnp.logical_not(some))
                def _():
                    for chunk in mine:
                        leave(chunk, state_ref[chunk])

                @pl.when(some & small)
                def _():
                    keeping(*mine)

                @pl.when(some & jnp.logical_not(small))
                def _():
                    lax.fori_loop(mine[0], mine[-1] + 1, lambda chunk, _: raising(chunk), None)

                return carry

            lax.fori_loop(0, chunks // group, body, 0)


def attend_own(qt, near, kv, part):
    chunks, dim, rows = qt.shape
    tok = kv.shape[0] // 2
    return pl.pallas_call(
        functools.partial(own_kernel, part=part),
        in_specs=[VMEM] * 3,
        out_specs=[VMEM] * 2,
        out_shape=[
            jax.ShapeDtypeStruct((chunks, dim + EXTRA, rows), f32),
            jax.ShapeDtypeStruct((8, 128), f32),
        ],
        scratch_shapes=[pltpu.VMEM((dim + EXTRA, tok), bf16)],
        compiler_params=PARAMS,
        cost_estimate=COST,
        name="attend_own",
    )(qt, near, kv)


def attend_earlier(qt, blocks, base, state, part, last=False):
    chunks, dim, rows = qt.shape
    width = len(blocks) * blocks[0].shape[0] // 2
    if last:
        out_shape = jax.ShapeDtypeStruct((chunks, part, rows // part * dim), bf16)
        out_specs, alias = VMEM, {}
    else:
        out_shape = [
            jax.ShapeDtypeStruct(state.shape, f32),
            jax.ShapeDtypeStruct((8, 128), f32),
        ]
        out_specs = [VMEM] * 2
        alias = {1 + len(blocks): 0}
    return pl.pallas_call(
        functools.partial(earlier_kernel, base=base, part=part, last=last),
        in_specs=[VMEM] * (2 + len(blocks)),
        out_specs=out_specs,
        out_shape=out_shape,
        input_output_aliases=alias,
        scratch_shapes=[
            pltpu.VMEM((width, dim), bf16),
            pltpu.VMEM((dim + EXTRA, width), bf16),
        ],
        compiler_params=PARAMS,
        cost_estimate=COST,
        name="attend_earlier",
    )(qt, *blocks, state)


def held_kernel(value_ref, after_ref, out_ref):
    out_ref[...] = value_ref[...]


def held(value, after):
    return pl.pallas_call(
        held_kernel,
        in_specs=[VMEM, ANY],
        out_specs=VMEM,
        out_shape=jax.ShapeDtypeStruct(value.shape, value.dtype),
        compiler_params=PARAMS,
        cost_estimate=COST,
        name="held",
    )(value, after)


def on_device(queries, keys, values, doc_ids):
    tok, heads, dim = queries.shape
    ring = lax.axis_size("kvh")
    part = tok // ring
    own_index = lax.axis_index("ctx")

    width = (SPAN + 1) * tok
    padded = jnp.concatenate([jnp.full((SPAN * tok,), -1, i32), doc_ids])
    near = lax.dynamic_slice_in_dim(padded, own_index * tok, width, 0).reshape(-1, 128)

    qt = queries.reshape(ring, part, heads, dim).transpose(0, 3, 2, 1)
    qt = qt.reshape(ring, dim, heads * part)

    kv0 = jnp.concatenate([keys[:, 0], values[:, 0]], 0)
    kv2 = hop(kv0, 2)
    kv1 = hop(held(kv0, qt), 1)
    state, done = attend_own(qt, near, kv0, part)
    kv4 = hop(held(kv2, done), 2)
    state, done = attend_earlier(qt, [kv2, kv1], 3 * tok, state, part)
    kv3 = hop(held(kv2, done), 1)
    kv5 = hop(held(kv4, done), 1)
    state, done = attend_earlier(qt, [kv4, kv3], tok, state, part)
    pieces = attend_earlier(qt, [kv5], 0, state, part, last=True)
    pieces = lax.all_to_all(pieces, "kvh", split_axis=0, concat_axis=0, tiled=True)
    return pieces.transpose(1, 0, 2).reshape(part, ring * heads * dim)


def solution(mesh):
    in_specs = (P("ctx", "kvh", None), P("ctx", "kvh", None), P("ctx", "kvh", None), P())
    out_specs = P(("ctx", "kvh"), None)
    return jax.shard_map(
        on_device, mesh=mesh, in_specs=in_specs, out_specs=out_specs, check_vma=False
    )
```
